32 devices in a mesh: shot: 2 (over y), slab: 8 (over z, x), side: 2 (over core).
Axes of the slice: x: 2, y: 2, z: 4, core: 2. Of those that a mesh axis runs over, the one named last changes fastest.
Arguments:
- field_now: float32 [256, 64, 128], P(('shot', 'slab'), 'side'), parts along dimension 0, may hold values from -6 to 6
- field_before: float32 [256, 64, 128], P(('shot', 'slab'), 'side'), parts along dimension 0, may hold values from -6 to 6
- courant: float32 [256, 64, 128], P(('shot', 'slab'), 'side'), parts along dimension 0, may hold values from 0.05 to 0.19
- wavelet: float32 [8], P('shot'), parts along dimension 0, may hold values from -60 to 60
- source_cell: int32 [2], P('shot'), parts along dimension 0, may hold values from 0 to 524287
- traces: float32 [8, 512], P('shot'), parts along dimension 0, may hold values from -60 to 60
- receiver_cells: int32 [1024], P('shot'), parts along dimension 0, may hold values from 0 to 524287
- offsets: int32 [64], P('shot'), parts along dimension 0, may hold values from 0 to 31, each once
Outputs:
- now_out: float32 [256, 64, 128], P(('shot', 'slab'), 'side'), parts along dimension 0
- before_out: float32 [256, 64, 128], P(('shot', 'slab'), 'side'), parts along dimension 0
- image: bfloat16 [256, 16, 64, 128], P(('shot', 'slab'), None, 'side'), parts along dimension 0
The draws below stay inside these ranges and needn't reach their ends.
There are 2 independent parts, one for each index of `shot`. The reference program is written for one: setup_inputs(seed, part) draws one part's arguments, and reference() takes and returns one part's arrays. A program takes and returns all parts, laid end to end along the dimension named above; each array names one. Nothing has to cross between parts.
Inputs may be any that keep to these rules, and one draw needn't show every extreme that they name: `offsets`: each value occurs exactly once.
All inputs are finite; a program needn't handle non-finite values.
Results may differ from the reference program's by a relative error of at most 0.001.
Values sent between devices are 32-bit elements; how exact they have to be, the bound alone decides.
A program may use at most 64 MiB of HBM per device.

```python
import jax
import jax.numpy as jnp
from jax import lax

NY = 128
LAGS = 32
STEPS = 4
NIMG = 2
NREC = 512
NZ = 64
NX = 64


def set_ends(result, key, smallest, top_value):
    longest = result.shape.index(max(result.shape))
    spots = []
    for shift in (0, 1):
        where = [jax.random.randint(jax.random.fold_in(key, axis), (), 0, length) for axis, length in enumerate(result.shape)]
        where[longest] = (where[longest] + shift) % result.shape[longest]
        spots.append(tuple(where))
    return result.at[spots[0]].set(smallest).at[spots[1]].set(top_value)


def level_of(own_key, shape, shards, least, top_value):
    factor_of = 1.0
    for position, blocks in shards:
        heights = jax.random.uniform(jax.random.fold_in(jax.random.fold_in(own_key, 6), position), (blocks,), jnp.float32, least / len(shards), top_value / len(shards))
        factor_of = factor_of * jnp.repeat(jnp.exp(heights), shape[position] // blocks).reshape((-1,) + (1,) * (len(shape) - 1 - position))
    return factor_of


def centred(key, shape, width, most, split=(), kind=jnp.bfloat16):
    values = jax.random.normal(key, shape, jnp.float32) * width
    if len(split) > 0:
        values = level_of(key, shape, split, -0.22, 0.18) * values
    return jnp.clip(values, min=-most, max=most).astype(kind)


def setup_inputs(seed: int = 0, part: int = 0) -> dict:
    arg_keys = jax.random.split(jax.random.key(seed), 9)
    part_keys = jax.random.split(jax.random.fold_in(arg_keys[8], part), 9)
    return {
        "field_now": centred(part_keys[0], (2 * NZ, NX, NY), 1.0, 6.0, ((0, 8), (1, 2)), jnp.float32),
        "field_before": centred(part_keys[1], (2 * NZ, NX, NY), 1.0, 6.0, ((0, 8), (1, 2)), jnp.float32),
        "courant": jnp.clip(0.05 + 0.14 * jax.random.uniform(part_keys[2], (2 * NZ, NX, NY), jnp.float32) ** level_of(part_keys[2], (2 * NZ, NX, NY), ((0, 8), (1, 2)), -0.2, 0.2), 0.05, 0.19),
        "wavelet": centred(part_keys[3], (STEPS,), 10.0, 60.0, (), jnp.float32),
        "source_cell": jax.random.randint(part_keys[4], (1,), 0, NZ * NX * NY).astype(jnp.int32),
        "traces": centred(part_keys[5], (STEPS, NREC), 10.0, 60.0, (), jnp.float32),
        "receiver_cells": set_ends(jax.random.randint(part_keys[6], (NREC,), 0, NZ * NX * NY), jax.random.fold_in(part_keys[6], 1), 0, (NZ * NX * NY) - 1).astype(jnp.int32),
        "offsets": jax.random.permutation(part_keys[7], LAGS).astype(jnp.int32),
    }


STENCIL_WEIGHTS = (-205.0 / 72.0, 8.0 / 5.0, -1.0 / 5.0, 8.0 / 315.0, -1.0 / 560.0)


def stencil(padded):
    depth = padded.shape[0] - 8
    across = padded.shape[1] - 8
    along = padded.shape[2] - 8
    center = padded[4:4 + depth, 4:4 + across, 4:4 + along]
    summed = (3.0 * STENCIL_WEIGHTS[0]) * center
    for reach in range(1, 5):
        pairs = padded[4 + reach:4 + reach + depth, 4:4 + across, 4:4 + along] + padded[4 - reach:4 - reach + depth, 4:4 + across, 4:4 + along]
        pairs = pairs + padded[4:4 + depth, 4 + reach:4 + reach + across, 4:4 + along] + padded[4:4 + depth, 4 - reach:4 - reach + across, 4:4 + along]
        pairs = pairs + padded[4:4 + depth, 4:4 + across, 4 + reach:4 + reach + along] + padded[4:4 + depth, 4:4 + across, 4 - reach:4 - reach + along]
        summed = summed + STENCIL_WEIGHTS[reach] * pairs
    return summed


def propagate(now, before, courant, cells, values):
    snapshots = []
    for instant in range(STEPS):
        impulse = jnp.zeros((now.size,), jnp.float32).at[cells].add(values[instant]).reshape(now.shape)
        laplace = stencil(jnp.pad(now, 4))
        later = 2.0 * now - before + courant * (laplace + impulse)
        before = now
        now = later
        snapshots.append(now)
    return now, before, jnp.stack(snapshots)


def source_rows(whole):
    return whole[NZ // 2:NZ // 2 + NZ]


def receiver_rows(whole):
    return jnp.concatenate([whole[3 * NZ // 2:], whole[:NZ // 2]], axis=0)


def combine(source_part, receiver_part):
    return jnp.concatenate([receiver_part[NZ // 2:], source_part, receiver_part[:NZ // 2]], axis=0)


def reference(field_now, field_before, courant, wavelet, source_cell, traces, receiver_cells, offsets):
    src_now, src_before, src_snaps = propagate(source_rows(field_now), source_rows(field_before), source_rows(courant), source_cell, wavelet[:, None])
    rec_now, rec_before, rec_snaps = propagate(receiver_rows(field_now), receiver_rows(field_before), receiver_rows(courant), receiver_cells, traces)
    margin = LAGS // 2
    picked = jnp.array([2 * j + 1 for j in range(NIMG)], jnp.int32)
    src_pick = jnp.take(jnp.pad(src_snaps, ((0, 0), (0, 0), (margin, margin), (0, 0))), picked, axis=0)
    rec_pick = jnp.take(jnp.pad(rec_snaps, ((0, 0), (0, 0), (margin, margin), (0, 0))), STEPS - 1 - picked, axis=0)
    slots = []
    for lag_slot in range(LAGS):
        offset_now = offsets[lag_slot] - margin
        s_piece = lax.dynamic_slice_in_dim(src_pick, (margin - offset_now).astype(jnp.int32), NX, 2)
        r_piece = lax.dynamic_slice_in_dim(rec_pick, (margin + offset_now).astype(jnp.int32), NX, 2)
        slots.append(jnp.sum(s_piece * r_piece, axis=0).astype(jnp.bfloat16))
    image = combine(jnp.stack(slots[:margin], axis=1), jnp.stack(slots[margin:], axis=1))
    now_out = combine(src_now, rec_now)
    before_out = combine(src_before, rec_before)
    return (now_out, before_out, image)
```

```python
import functools

import jax
import jax.numpy as jnp
from jax import lax
from jax.experimental import pallas as pl
from jax.experimental.pallas import tpu as pltpu
from jax.sharding import PartitionSpec as P

LAGS = 32
STEPS = 4
MARGIN = LAGS // 2
REACH = 4
CHUNKS = 4
STENCIL_WEIGHTS = (-205.0 / 72.0, 8.0 / 5.0, -1.0 / 5.0, 8.0 / 315.0, -1.0 / 560.0)
MESH = pl.DeviceIdType.MESH


def split_bf16(value):
    high = value.astype(jnp.bfloat16)
    low = (value - high.astype(jnp.float32)).astype(jnp.bfloat16)
    return high, low


def kernel(
    slabs,
    now_ref, before_ref, courant_ref, traces_ref, cells_ref, wavelet_ref, source_ref, offsets_ref,
    now_out, before_out, image_ref,
    p0, p1, p2, p3, p4, qa, qb0, qb1, qb2, qb3, impulse, partial,
    low_send, low_recv, high_send, high_recv, side_send, side_recv,
    pair_send, pair_recv, fwd_send, fwd_recv,
):
    depth, cols, along = now_ref.shape
    fields = [p0, p1, p2, p3, p4]
    qb = [qb0, qb1, qb2, qb3]
    part = depth // CHUNKS
    inner = pl.ds(MARGIN, cols)
    shot = lax.axis_index("shot")
    slab = lax.axis_index("slab")
    side = lax.axis_index("side")
    quarter = slabs // 4
    is_receiver = (slab < quarter) | (slab >= 3 * quarter)
    is_source = jnp.logical_not(is_receiver)
    has_low = (slab != quarter) & (slab != 3 * quarter)
    has_high = (slab != quarter - 1) & (slab != 3 * quarter - 1)
    low = (shot, lax.rem(slab + slabs - 1, slabs), side)
    high = (shot, lax.rem(slab + 1, slabs), side)
    partner = (shot, lax.rem(slab + 2 * quarter, slabs), side)
    peer = (shot, slab, 1 - side)

    def low_copy(step):
        return pltpu.make_async_remote_copy(
            src_ref=fields[step].at[pl.ds(REACH, REACH), inner],
            dst_ref=fields[step].at[pl.ds(REACH + depth, REACH), inner],
            send_sem=low_send.at[step], recv_sem=low_recv.at[step],
            device_id=low, device_id_type=MESH,
        )

    def high_copy(step):
        return pltpu.make_async_remote_copy(
            src_ref=fields[step].at[pl.ds(depth, REACH), inner],
            dst_ref=fields[step].at[pl.ds(0, REACH), inner],
            send_sem=high_send.at[step], recv_sem=high_recv.at[step],
            device_id=high, device_id_type=MESH,
        )

    side_from = pl.multiple_of(jnp.where(side == 0, cols, MARGIN), 8)
    side_to = pl.multiple_of(jnp.where(side == 0, 0, MARGIN + cols), 8)

    def side_copy(step):
        rows = pl.ds(REACH, depth)
        return pltpu.make_async_remote_copy(
            src_ref=fields[step].at[rows, pl.ds(side_from, MARGIN)],
            dst_ref=fields[step].at[rows, pl.ds(side_to, MARGIN)],
            send_sem=side_send.at[step], recv_sem=side_recv.at[step],
            device_id=peer, device_id_type=MESH,
        )

    def pair_copies(step, second):
        if not second:
            return [pltpu.make_async_remote_copy(
                src_ref=fields[step].at[pl.ds(REACH, depth), inner],
                dst_ref=qa.at[:, inner],
                send_sem=pair_send.at[CHUNKS], recv_sem=pair_recv.at[CHUNKS],
                device_id=partner, device_id_type=MESH,
            )]
        return [pltpu.make_async_remote_copy(
            src_ref=fields[step].at[pl.ds(REACH + c * part, part), inner],
            dst_ref=qb[c].at[:, inner],
            send_sem=pair_send.at[c], recv_sem=pair_recv.at[c],
            device_id=partner, device_id_type=MESH,
        ) for c in range(CHUNKS)]

    def forward(ref, index):
        return pltpu.make_async_remote_copy(
            src_ref=ref.at[:, pl.ds(side_from, MARGIN)],
            dst_ref=ref.at[:, pl.ds(side_to, MARGIN)],
            send_sem=fwd_send.at[index], recv_sem=fwd_recv.at[index],
            device_id=peer, device_id_type=MESH,
        )

    def clear(ref, pads):
        rows, width = ref.shape[0], ref.shape[1]

        def body(z, carry):
            ref[z, 0:MARGIN] = jnp.zeros((MARGIN, along), jnp.float32)
            ref[z, width - MARGIN : width] = jnp.zeros((MARGIN, along), jnp.float32)
            return carry

        lax.fori_loop(0, rows, body, 0)
        if pads:
            for z in list(range(REACH)) + list(range(rows - REACH, rows)):
                ref[z, inner] = jnp.zeros((cols, along), jnp.float32)

    def load_now(z, carry):
        p0[REACH + z, inner] = now_ref[z]
        return carry

    lax.fori_loop(0, depth, load_now, 0)
    for ref in fields:
        clear(ref, ref is not p4)
    for ref in [qa] + qb:
        clear(ref, False)

    barrier = pltpu.get_barrier_semaphore()
    pl.semaphore_signal(barrier, inc=1, device_id=peer, device_id_type=MESH)
    pl.semaphore_signal(barrier, inc=1, device_id=partner, device_id_type=MESH)

    @pl.when(has_low)
    def _():
        pl.semaphore_signal(barrier, inc=1, device_id=low, device_id_type=MESH)

    @pl.when(has_high)
    def _():
        pl.semaphore_signal(barrier, inc=1, device_id=high, device_id_type=MESH)

    pl.semaphore_wait(
        barrier, 2 + jnp.where(has_low, 1, 0) + jnp.where(has_high, 1, 0)
    )

    def start_depth(step):
        @pl.when(has_low)
        def _():
            low_copy(step).start()

        @pl.when(has_high)
        def _():
            high_copy(step).start()

    start_depth(0)
    side_copy(0).start()

    count = cells_ref.shape[1]
    first_lane = lax.broadcasted_iota(jnp.int32, (1, count), 1) == 0
    cells = jnp.where(
        is_receiver, cells_ref[...], jnp.where(first_lane, source_ref[0], -1)
    )
    depth_start = jnp.where(
        is_receiver, lax.rem(slab + quarter, slabs), slab - quarter
    ) * depth
    cols_all = 2 * cols
    safe = jnp.maximum(cells, 0)
    cell_depth = lax.div(safe, cols_all * along) - depth_start
    cell_across = lax.rem(lax.div(safe, along), cols_all) - side * cols
    cell_along = lax.rem(safe, along)
    inside = (
        (cells >= 0) & (cell_depth >= 0) & (cell_depth < depth)
        & (cell_across >= 0) & (cell_across < cols)
    )
    cell_row = jnp.where(inside, cell_depth * cols + cell_across, -1)
    row_hot = jnp.where(
        lax.broadcasted_iota(jnp.int32, (depth * cols, count), 0) == cell_row, 1.0, 0.0
    ).astype(jnp.bfloat16)
    along_hot = lax.broadcasted_iota(jnp.int32, (along, count), 0) == cell_along
    over_cells = (((1,), (1,)), ((), ()))
    for step in range(STEPS):
        amount = jnp.where(
            is_receiver,
            traces_ref[step : step + 1, :],
            jnp.where(first_lane, wavelet_ref[step], 0.0),
        )
        spread_high, spread_low = split_bf16(jnp.where(along_hot, amount, 0.0))
        both = lax.dot_general(
            row_hot, spread_high, over_cells, preferred_element_type=jnp.float32
        ) + lax.dot_general(
            row_hot, spread_low, over_cells, preferred_element_type=jnp.float32
        )
        impulse[step] = both.reshape(depth, cols, along)

    apart = jnp.abs(
        lax.broadcasted_iota(jnp.int32, (along, along), 0)
        - lax.broadcasted_iota(jnp.int32, (along, along), 1)
    )
    band = jnp.where(apart == 0, 3.0 * STENCIL_WEIGHTS[0], 0.0)
    for reach in range(1, REACH + 1):
        band = jnp.where(apart == reach, STENCIL_WEIGHTS[reach], band)
    band_high, band_low = split_bf16(band)

    def advance(step, first):
        field, later = fields[step], fields[step + 1]
        zs = pl.ds(first, part)
        centre = field[pl.ds(first + REACH, part), inner]
        c_high, c_low = split_bf16(centre.reshape(part * cols, along))
        summed = (
            jnp.dot(c_high, band_high, preferred_element_type=jnp.float32)
            + jnp.dot(c_low, band_high, preferred_element_type=jnp.float32)
            + jnp.dot(c_high, band_low, preferred_element_type=jnp.float32)
        ).reshape(part, cols, along)
        for reach in range(1, REACH + 1):
            pairs = (
                field[pl.ds(first + REACH + reach, part), inner]
                + field[pl.ds(first + REACH - reach, part), inner]
            ) + (
                field[pl.ds(first + REACH, part), MARGIN + reach : MARGIN + reach + cols]
                + field[pl.ds(first + REACH, part), MARGIN - reach : MARGIN - reach + cols]
            )
            summed = summed + STENCIL_WEIGHTS[reach] * pairs
        if step == 0:
            before = before_ref[zs]
        else:
            before = fields[step - 1][pl.ds(first + REACH, part), inner]
        result = 2.0 * centre - before + courant_ref[zs] * (summed + impulse[step, zs])
        later[pl.ds(first + REACH, part), inner] = result
        if step == STEPS - 1:
            now_out[zs] = result
            before_out[zs] = centre

    for step in range(STEPS):
        side_copy(step).wait_recv()

        def body(c, carry, step=step):
            advance(step, c * part)
            return carry

        lax.fori_loop(1, CHUNKS - 1, body, 0)

        @pl.when(has_high)
        def _():
            low_copy(step).wait_recv()

        @pl.when(has_low)
        def _():
            high_copy(step).wait_recv()

        def edge(c, carry, step=step):
            advance(step, c * (depth - part))
            return carry

        lax.fori_loop(0, 2, edge, 0)
        if step < STEPS - 1:
            start_depth(step + 1)
        side_copy(step + 1).start()

        @pl.when(is_source if step % 2 else is_receiver)
        def _():
            for copy in pair_copies(step + 1, step >= 2):
                copy.start()

    side_copy(STEPS).wait_recv()
    pair_copies(1, False)[0].wait_recv()
    forward(qa, CHUNKS).start()
    forward(qa, CHUNKS).wait_recv()
    slot_base = jnp.where(is_receiver, MARGIN, 0)
    sign = jnp.where(is_receiver, 1, -1)

    def starts(slot):
        lag = (offsets_ref[slot_base + slot] - MARGIN) * sign
        return MARGIN + lag, MARGIN - lag

    def first_product(own):
        def body(slot, carry):
            own_at, other_at = starts(slot)
            for z in range(depth):
                partial[z, slot] = (
                    own[REACH + z, pl.ds(own_at, cols)] * qa[z, pl.ds(other_at, cols)]
                )
            return carry

        lax.fori_loop(0, MARGIN, body, 0)

    def last_product(own, c):
        def body(slot, carry):
            own_at, other_at = starts(slot)
            for z in range(part):
                row = c * part + z
                image_ref[row, slot] = (
                    partial[row, slot]
                    + own[REACH + row, pl.ds(own_at, cols)]
                    * qb[c][z, pl.ds(other_at, cols)]
                ).astype(jnp.bfloat16)
            return carry

        lax.fori_loop(0, MARGIN, body, 0)

    @pl.when(is_source)
    def _():
        first_product(p4)

    @pl.when(is_receiver)
    def _():
        first_product(p3)

    seconds = pair_copies(3, True)
    seconds[0].wait_recv()
    forward(qb[0], 0).start()
    for c in range(CHUNKS):
        if c + 1 < CHUNKS:
            seconds[c + 1].wait_recv()
            forward(qb[c + 1], c + 1).start()
        forward(qb[c], c).wait_recv()

        @pl.when(is_source)
        def _():
            last_product(p2, c)

        @pl.when(is_receiver)
        def _():
            last_product(p1, c)

    for step in range(STEPS):
        @pl.when(has_low)
        def _():
            low_copy(step).wait_send()

        @pl.when(has_high)
        def _():
            high_copy(step).wait_send()

    for step in range(STEPS + 1):
        side_copy(step).wait_send()
    pair_copies(1, False)[0].wait_send()
    for c in range(CHUNKS):
        seconds[c].wait_send()
        forward(qb[c], c).wait_send()
    forward(qa, CHUNKS).wait_send()


def shards(field_now, field_before, courant, wavelet, source_cell, traces, receiver_cells, offsets):
    depth, cols, along = field_now.shape
    f32 = jnp.float32
    vmem = pl.BlockSpec(memory_space=pltpu.VMEM)
    smem = pl.BlockSpec(memory_space=pltpu.SMEM)
    field = pltpu.VMEM((depth + 2 * REACH, cols + 2 * MARGIN, along), f32)
    part = depth // CHUNKS
    dma = pltpu.SemaphoreType.DMA
    return pl.pallas_call(
        functools.partial(kernel, lax.axis_size("slab")),
        out_shape=(
            jax.ShapeDtypeStruct(field_now.shape, f32),
            jax.ShapeDtypeStruct(field_now.shape, f32),
            jax.ShapeDtypeStruct((depth, MARGIN, cols, along), jnp.bfloat16),
        ),
        in_specs=[vmem] * 5 + [smem] * 3,
        out_specs=(vmem, vmem, vmem),
        scratch_shapes=[field] * 5
        + [pltpu.VMEM((depth, cols + 2 * MARGIN, along), f32)]
        + [pltpu.VMEM((part, cols + 2 * MARGIN, along), f32)] * CHUNKS
        + [
            pltpu.VMEM((STEPS, depth, cols, along), f32),
            pltpu.VMEM((depth, MARGIN, cols, along), f32),
            dma((STEPS,)), dma((STEPS,)), dma((STEPS,)), dma((STEPS,)),
            dma((STEPS + 1,)), dma((STEPS + 1,)),
            dma((CHUNKS + 1,)), dma((CHUNKS + 1,)), dma((CHUNKS + 1,)), dma((CHUNKS + 1,)),
        ],
        compiler_params=pltpu.CompilerParams(
            collective_id=0, has_side_effects=True, vmem_limit_bytes=40 * 1024 * 1024
        ),
    )(
        field_now, field_before, courant, traces, receiver_cells.reshape(1, -1),
        wavelet, source_cell, offsets,
    )


def solution(mesh):
    return jax.shard_map(
        shards,
        mesh=mesh,
        in_specs=(
            P(("shot", "slab"), "side", None),
            P(("shot", "slab"), "side", None),
            P(("shot", "slab"), "side", None),
            P("shot"),
            P("shot"),
            P("shot", None),
            P("shot"),
            P("shot"),
        ),
        out_specs=(
            P(("shot", "slab"), "side", None),
            P(("shot", "slab"), "side", None),
            P(("shot", "slab"), None, "side", None),
        ),
        check_vma=False,
    )
```

```python
import functools

import jax
import jax.numpy as jnp
from jax import lax
from jax.experimental import pallas as pl
from jax.experimental.pallas import tpu as pltpu
from jax.sharding import PartitionSpec as P

LAGS = 32
STEPS = 4
MARGIN = LAGS // 2
REACH = 4
CHUNKS = 4
STENCIL_WEIGHTS = (-205.0 / 72.0, 8.0 / 5.0, -1.0 / 5.0, 8.0 / 315.0, -1.0 / 560.0)
MESH = pl.DeviceIdType.MESH


def split_bf16(value):
    high = value.astype(jnp.bfloat16)
    low = (value - high.astype(jnp.float32)).astype(jnp.bfloat16)
    return high, low


def kernel(
    slabs,
    now_hbm, before_hbm, courant_hbm, traces_hbm, cells_hbm, wavelet_hbm, source_hbm, offsets_hbm,
    now_out, before_out, image_out,
    p0, p1, p2, p3, p4, qa, qb0, qb1, qb2, qb3, impulse, partial,
    before_ref, courant_ref, traces_ref, cells_ref, wavelet_ref, source_ref, offsets_ref, load_sem,
    image_ref, store_sem,
    low_send, low_recv, high_send, high_recv, side_send, side_recv,
    pair_send, pair_recv, fwd_send, fwd_recv,
):
    depth, cols, along = now_hbm.shape
    fields = [p0, p1, p2, p3, p4]
    qb = [qb0, qb1, qb2, qb3]
    part = depth // CHUNKS
    inner = pl.ds(MARGIN, cols)
    shot = lax.axis_index("shot")
    slab = lax.axis_index("slab")
    side = lax.axis_index("side")
    quarter = slabs // 4
    is_receiver = (slab < quarter) | (slab >= 3 * quarter)
    is_source = jnp.logical_not(is_receiver)
    has_low = (slab != quarter) & (slab != 3 * quarter)
    has_high = (slab != quarter - 1) & (slab != 3 * quarter - 1)
    low = (shot, lax.rem(slab + slabs - 1, slabs), side)
    high = (shot, lax.rem(slab + 1, slabs), side)
    partner = (shot, lax.rem(slab + 2 * quarter, slabs), side)
    peer = (shot, slab, 1 - side)

    loads = [
        pltpu.make_async_copy(source, target, load_sem.at[index])
        for index, (source, target) in enumerate((
            (now_hbm, p0.at[pl.ds(REACH, depth), inner]),
            (cells_hbm, cells_ref), (traces_hbm, traces_ref),
            (wavelet_hbm, wavelet_ref), (source_hbm, source_ref),
            (before_hbm, before_ref), (courant_hbm, courant_ref), (offsets_hbm, offsets_ref),
        ))
    ]
    for load in loads:
        load.start()

    def low_copy(step):
        return pltpu.make_async_remote_copy(
            src_ref=fields[step].at[pl.ds(REACH, REACH), inner],
            dst_ref=fields[step].at[pl.ds(REACH + depth, REACH), inner],
            send_sem=low_send.at[step], recv_sem=low_recv.at[step],
            device_id=low, device_id_type=MESH,
        )

    def high_copy(step):
        return pltpu.make_async_remote_copy(
            src_ref=fields[step].at[pl.ds(depth, REACH), inner],
            dst_ref=fields[step].at[pl.ds(0, REACH), inner],
            send_sem=high_send.at[step], recv_sem=high_recv.at[step],
            device_id=high, device_id_type=MESH,
        )

    side_from = pl.multiple_of(jnp.where(side == 0, cols, MARGIN), 8)
    side_to = pl.multiple_of(jnp.where(side == 0, 0, MARGIN + cols), 8)

    def side_copy(step):
        rows = pl.ds(REACH, depth)
        return pltpu.make_async_remote_copy(
            src_ref=fields[step].at[rows, pl.ds(side_from, MARGIN)],
            dst_ref=fields[step].at[rows, pl.ds(side_to, MARGIN)],
            send_sem=side_send.at[step], recv_sem=side_recv.at[step],
            device_id=peer, device_id_type=MESH,
        )

    def pair_copies(step, second):
        if not second:
            return [pltpu.make_async_remote_copy(
                src_ref=fields[step].at[pl.ds(REACH + first, rows), inner],
                dst_ref=qa.at[pl.ds(first, rows), inner],
                send_sem=pair_send.at[CHUNKS + index], recv_sem=pair_recv.at[CHUNKS + index],
                device_id=partner, device_id_type=MESH,
            ) for index, (first, rows) in enumerate(
                ((part, depth - 2 * part), (0, part), (depth - part, part))
            )]
        return [pltpu.make_async_remote_copy(
            src_ref=fields[step].at[pl.ds(REACH + c * part, part), inner],
            dst_ref=qb[c].at[:, inner],
            send_sem=pair_send.at[c], recv_sem=pair_recv.at[c],
            device_id=partner, device_id_type=MESH,
        ) for c in range(CHUNKS)]

    def forward(ref, index):
        return pltpu.make_async_remote_copy(
            src_ref=ref.at[:, pl.ds(side_from, MARGIN)],
            dst_ref=ref.at[:, pl.ds(side_to, MARGIN)],
            send_sem=fwd_send.at[index], recv_sem=fwd_recv.at[index],
            device_id=peer, device_id_type=MESH,
        )

    def clear(ref, pads):
        rows, width = ref.shape[0], ref.shape[1]

        def body(z, carry):
            ref[z, 0:MARGIN] = jnp.zeros((MARGIN, along), jnp.float32)
            ref[z, width - MARGIN : width] = jnp.zeros((MARGIN, along), jnp.float32)
            return carry

        lax.fori_loop(0, rows, body, 0)
        if pads:
            for z in list(range(REACH)) + list(range(rows - REACH, rows)):
                ref[z, inner] = jnp.zeros((cols, along), jnp.float32)

    for ref in fields:
        clear(ref, ref is not p4)
    for ref in [qa] + qb:
        clear(ref, False)

    barrier = pltpu.get_barrier_semaphore()
    pl.semaphore_signal(barrier, inc=1, device_id=peer, device_id_type=MESH)
    pl.semaphore_signal(barrier, inc=1, device_id=partner, device_id_type=MESH)

    @pl.when(has_low)
    def _():
        pl.semaphore_signal(barrier, inc=1, device_id=low, device_id_type=MESH)

    @pl.when(has_high)
    def _():
        pl.semaphore_signal(barrier, inc=1, device_id=high, device_id_type=MESH)

    pl.semaphore_wait(
        barrier, 2 + jnp.where(has_low, 1, 0) + jnp.where(has_high, 1, 0)
    )

    def start_depth(step):
        @pl.when(has_low)
        def _():
            low_copy(step).start()

        @pl.when(has_high)
        def _():
            high_copy(step).start()

    loads[0].wait()
    start_depth(0)
    side_copy(0).start()

    for load in loads[1:5]:
        load.wait()

    count = cells_ref.shape[1]
    first_lane = lax.broadcasted_iota(jnp.int32, (1, count), 1) == 0
    cells = jnp.where(
        is_receiver, cells_ref[...], jnp.where(first_lane, source_ref[0], -1)
    )
    depth_start = jnp.where(
        is_receiver, lax.rem(slab + quarter, slabs), slab - quarter
    ) * depth
    cols_all = 2 * cols
    safe = jnp.maximum(cells, 0)
    cell_depth = lax.div(safe, cols_all * along) - depth_start
    cell_across = lax.rem(lax.div(safe, along), cols_all) - side * cols
    cell_along = lax.rem(safe, along)
    inside = (
        (cells >= 0) & (cell_depth >= 0) & (cell_depth < depth)
        & (cell_across >= 0) & (cell_across < cols)
    )
    cell_row = jnp.where(inside, cell_depth * cols + cell_across, -1)
    row_hot = jnp.where(
        lax.broadcasted_iota(jnp.int32, (depth * cols, count), 0) == cell_row, 1.0, 0.0
    ).astype(jnp.bfloat16)
    along_hot = lax.broadcasted_iota(jnp.int32, (along, count), 0) == cell_along
    over_cells = (((1,), (1,)), ((), ()))

    def make_impulse(step):
        amount = jnp.where(
            is_receiver,
            traces_ref[step : step + 1, :],
            jnp.where(first_lane, wavelet_ref[step], 0.0),
        )
        spread = jnp.concatenate(split_bf16(jnp.where(along_hot, amount, 0.0)), axis=0)
        both = lax.dot_general(row_hot, spread, over_cells, preferred_element_type=jnp.float32)
        impulse[step] = (both[:, :along] + both[:, along:]).reshape(depth, cols, along)

    make_impulse(0)

    apart = jnp.abs(
        lax.broadcasted_iota(jnp.int32, (along, along), 0)
        - lax.broadcasted_iota(jnp.int32, (along, along), 1)
    )
    band = jnp.where(apart == 0, 3.0 * STENCIL_WEIGHTS[0], 0.0)
    for reach in range(1, REACH + 1):
        band = jnp.where(apart == reach, STENCIL_WEIGHTS[reach], band)
    band_high, band_low = split_bf16(band)

    def advance(step, first):
        field, later = fields[step], fields[step + 1]
        zs = pl.ds(first, part)
        centre = field[pl.ds(first + REACH, part), inner]
        c_high, c_low = split_bf16(centre.reshape(part * cols, along))
        summed = (
            jnp.dot(c_high, band_high, preferred_element_type=jnp.float32)
            + jnp.dot(c_low, band_high, preferred_element_type=jnp.float32)
            + jnp.dot(c_high, band_low, preferred_element_type=jnp.float32)
        ).reshape(part, cols, along)
        for reach in range(1, REACH + 1):
            pairs = (
                field[pl.ds(first + REACH + reach, part), inner]
                + field[pl.ds(first + REACH - reach, part), inner]
            ) + (
                field[pl.ds(first + REACH, part), MARGIN + reach : MARGIN + reach + cols]
                + field[pl.ds(first + REACH, part), MARGIN - reach : MARGIN - reach + cols]
            )
            summed = summed + STENCIL_WEIGHTS[reach] * pairs
        if step == 0:
            before = before_ref[zs]
        else:
            before = fields[step - 1][pl.ds(first + REACH, part), inner]
        result = 2.0 * centre - before + courant_ref[zs] * (summed + impulse[step, zs])
        later[pl.ds(first + REACH, part), inner] = result

    for load in loads[5:]:
        load.wait()
    for step in range(STEPS):
        side_copy(step).wait_recv()

        def body(c, carry, step=step):
            advance(step, c * part)
            return carry

        lax.fori_loop(1, CHUNKS - 1, body, 0)

        sends_pair = is_source if step % 2 else is_receiver
        copies = pair_copies(step + 1, step >= 2)
        if step < 2:
            @pl.when(sends_pair)
            def _():
                copies[0].start()

        @pl.when(has_high)
        def _():
            low_copy(step).wait_recv()

        @pl.when(has_low)
        def _():
            high_copy(step).wait_recv()

        def edge(c, carry, step=step):
            advance(step, c * (depth - part))
            return carry

        lax.fori_loop(0, 2, edge, 0)
        if step < STEPS - 1:
            start_depth(step + 1)
        side_copy(step + 1).start()

        @pl.when(sends_pair)
        def _():
            for copy in copies[1:] if step < 2 else copies:
                copy.start()

        if step == 0:
            for later_step in range(1, STEPS):
                make_impulse(later_step)

    stores = [
        pltpu.make_async_copy(
            ref.at[pl.ds(REACH, depth), inner], target, store_sem.at[CHUNKS + index]
        )
        for index, (ref, target) in enumerate(((p4, now_out), (p3, before_out)))
    ]
    for store in stores:
        store.start()
    side_copy(STEPS).wait_recv()
    for copy in pair_copies(1, False):
        copy.wait_recv()
    forward(qa, CHUNKS).start()
    forward(qa, CHUNKS).wait_recv()
    slot_base = jnp.where(is_receiver, MARGIN, 0)
    sign = jnp.where(is_receiver, 1, -1)

    def starts(slot):
        lag = (offsets_ref[slot_base + slot] - MARGIN) * sign
        return MARGIN + lag, MARGIN - lag

    def first_product(own):
        def body(slot, carry):
            own_at, other_at = starts(slot)
            for z in range(depth):
                partial[z, slot] = (
                    own[REACH + z, pl.ds(own_at, cols)] * qa[z, pl.ds(other_at, cols)]
                )
            return carry

        lax.fori_loop(0, MARGIN, body, 0)

    def last_product(own, c):
        def body(slot, carry):
            own_at, other_at = starts(slot)
            for z in range(part):
                row = c * part + z
                image_ref[row, slot] = (
                    partial[row, slot]
                    + own[REACH + row, pl.ds(own_at, cols)]
                    * qb[c][z, pl.ds(other_at, cols)]
                ).astype(jnp.bfloat16)
            return carry

        lax.fori_loop(0, MARGIN, body, 0)

    @pl.when(is_source)
    def _():
        first_product(p4)

    @pl.when(is_receiver)
    def _():
        first_product(p3)

    seconds = pair_copies(3, True)
    seconds[0].wait_recv()
    forward(qb[0], 0).start()
    for c in range(CHUNKS):
        if c + 1 < CHUNKS:
            seconds[c + 1].wait_recv()
            forward(qb[c + 1], c + 1).start()
        forward(qb[c], c).wait_recv()

        @pl.when(is_source)
        def _():
            last_product(p2, c)

        @pl.when(is_receiver)
        def _():
            last_product(p1, c)

        rows = pl.ds(c * part, part)
        stores.append(
            pltpu.make_async_copy(image_ref.at[rows], image_out.at[rows], store_sem.at[c])
        )
        stores[-1].start()

    for store in stores:
        store.wait()
    for step in range(STEPS):
        @pl.when(has_low)
        def _():
            low_copy(step).wait_send()

        @pl.when(has_high)
        def _():
            high_copy(step).wait_send()

    for step in range(STEPS + 1):
        side_copy(step).wait_send()
    for copy in pair_copies(1, False):
        copy.wait_send()
    for c in range(CHUNKS):
        seconds[c].wait_send()
        forward(qb[c], c).wait_send()
    forward(qa, CHUNKS).wait_send()


def shards(field_now, field_before, courant, wavelet, source_cell, traces, receiver_cells, offsets):
    depth, cols, along = field_now.shape
    f32 = jnp.float32
    hbm = pl.BlockSpec(memory_space=pltpu.HBM)
    i32 = jnp.int32
    field = pltpu.VMEM((depth + 2 * REACH, cols + 2 * MARGIN, along), f32)
    part = depth // CHUNKS
    dma = pltpu.SemaphoreType.DMA
    return pl.pallas_call(
        functools.partial(kernel, lax.axis_size("slab")),
        out_shape=(
            jax.ShapeDtypeStruct(field_now.shape, f32),
            jax.ShapeDtypeStruct(field_now.shape, f32),
            jax.ShapeDtypeStruct((depth, MARGIN, cols, along), jnp.bfloat16),
        ),
        in_specs=[hbm] * 8,
        out_specs=(hbm, hbm, hbm),
        scratch_shapes=[field] * 5
        + [pltpu.VMEM((depth, cols + 2 * MARGIN, along), f32)]
        + [pltpu.VMEM((part, cols + 2 * MARGIN, along), f32)] * CHUNKS
        + [
            pltpu.VMEM((STEPS, depth, cols, along), f32),
            pltpu.VMEM((depth, MARGIN, cols, along), f32),
            pltpu.VMEM(field_now.shape, f32), pltpu.VMEM(field_now.shape, f32),
            pltpu.VMEM(traces.shape, f32), pltpu.VMEM((1, receiver_cells.shape[0]), i32),
            pltpu.SMEM(wavelet.shape, f32), pltpu.SMEM(source_cell.shape, i32),
            pltpu.SMEM(offsets.shape, i32), dma((8,)),
            pltpu.VMEM((depth, MARGIN, cols, along), jnp.bfloat16), dma((CHUNKS + 2,)),
            dma((STEPS,)), dma((STEPS,)), dma((STEPS,)), dma((STEPS,)),
            dma((STEPS + 1,)), dma((STEPS + 1,)),
            dma((CHUNKS + 3,)), dma((CHUNKS + 3,)), dma((CHUNKS + 1,)), dma((CHUNKS + 1,)),
        ],
        compiler_params=pltpu.CompilerParams(
            collective_id=0, has_side_effects=True, vmem_limit_bytes=61 * 1024 * 1024
        ),
    )(
        field_now, field_before, courant, traces, receiver_cells.reshape(1, -1),
        wavelet, source_cell, offsets,
    )


def solution(mesh):
    return jax.shard_map(
        shards,
        mesh=mesh,
        in_specs=(
            P(("shot", "slab"), "side", None),
            P(("shot", "slab"), "side", None),
            P(("shot", "slab"), "side", None),
            P("shot"),
            P("shot"),
            P("shot", None),
            P("shot"),
            P("shot"),
        ),
        out_specs=(
            P(("shot", "slab"), "side", None),
            P(("shot", "slab"), "side", None),
            P(("shot", "slab"), None, "side", None),
        ),
        check_vma=False,
    )
```

```python
import functools

import jax
import jax.numpy as jnp
from jax import lax
from jax.experimental import pallas as pl
from jax.experimental.pallas import tpu as pltpu
from jax.sharding import PartitionSpec as P

LAGS = 32
STEPS = 4
MARGIN = LAGS // 2
REACH = 4
CHUNKS = 4
STENCIL_WEIGHTS = (-205.0 / 72.0, 8.0 / 5.0, -1.0 / 5.0, 8.0 / 315.0, -1.0 / 560.0)
MESH = pl.DeviceIdType.MESH


def split_bf16(value):
    high = value.astype(jnp.bfloat16)
    low = (value - high.astype(jnp.float32)).astype(jnp.bfloat16)
    return high, low


def kernel(
    slabs,
    now_hbm, before_hbm, courant_hbm, traces_hbm, cells_hbm, wavelet_hbm, source_hbm, offsets_hbm,
    now_out, before_out, image_out,
    p0, p1, p2, p3, p4, qa, qb0, qb1, qb2, qb3, impulse, partial,
    before_ref, courant_ref, traces_ref, cells_ref, wavelet_ref, source_ref, offsets_ref, load_sem,
    image_ref, store_sem,
    low_send, low_recv, high_send, high_recv, side_send, side_recv,
    pair_send, pair_recv, fwd_send, fwd_recv,
):
    depth, cols, along = now_hbm.shape
    fields = [p0, p1, p2, p3, p4]
    qb = [qb0, qb1, qb2, qb3]
    part = depth // CHUNKS
    inner = pl.ds(MARGIN, cols)
    shot = lax.axis_index("shot")
    slab = lax.axis_index("slab")
    side = lax.axis_index("side")
    quarter = slabs // 4
    is_receiver = (slab < quarter) | (slab >= 3 * quarter)
    is_source = jnp.logical_not(is_receiver)
    has_low = (slab != quarter) & (slab != 3 * quarter)
    has_high = (slab != quarter - 1) & (slab != 3 * quarter - 1)
    low = (shot, lax.rem(slab + slabs - 1, slabs), side)
    high = (shot, lax.rem(slab + 1, slabs), side)
    partner = (shot, lax.rem(slab + 2 * quarter, slabs), side)
    peer = (shot, slab, 1 - side)

    loads = [
        pltpu.make_async_copy(source, target, load_sem.at[index])
        for index, (source, target) in enumerate((
            (now_hbm, p0.at[pl.ds(REACH, depth), inner]),
            (cells_hbm, cells_ref), (traces_hbm, traces_ref),
            (wavelet_hbm, wavelet_ref), (source_hbm, source_ref),
            (before_hbm, before_ref), (courant_hbm, courant_ref), (offsets_hbm, offsets_ref),
        ))
    ]
    for load in loads:
        load.start()

    def low_copy(step):
        return pltpu.make_async_remote_copy(
            src_ref=fields[step].at[pl.ds(REACH, REACH), inner],
            dst_ref=fields[step].at[pl.ds(REACH + depth, REACH), inner],
            send_sem=low_send.at[step], recv_sem=low_recv.at[step],
            device_id=low, device_id_type=MESH,
        )

    def high_copy(step):
        return pltpu.make_async_remote_copy(
            src_ref=fields[step].at[pl.ds(depth, REACH), inner],
            dst_ref=fields[step].at[pl.ds(0, REACH), inner],
            send_sem=high_send.at[step], recv_sem=high_recv.at[step],
            device_id=high, device_id_type=MESH,
        )

    side_from = pl.multiple_of(jnp.where(side == 0, cols, MARGIN), 8)
    side_to = pl.multiple_of(jnp.where(side == 0, 0, MARGIN + cols), 8)

    def side_copy(step):
        rows = pl.ds(REACH, depth)
        return pltpu.make_async_remote_copy(
            src_ref=fields[step].at[rows, pl.ds(side_from, MARGIN)],
            dst_ref=fields[step].at[rows, pl.ds(side_to, MARGIN)],
            send_sem=side_send.at[step], recv_sem=side_recv.at[step],
            device_id=peer, device_id_type=MESH,
        )

    def pair_copies(step, second):
        if not second:
            return [pltpu.make_async_remote_copy(
                src_ref=fields[step].at[pl.ds(REACH + first, rows), inner],
                dst_ref=qa.at[pl.ds(first, rows), inner],
                send_sem=pair_send.at[CHUNKS + index], recv_sem=pair_recv.at[CHUNKS + index],
                device_id=partner, device_id_type=MESH,
            ) for index, (first, rows) in enumerate(
                ((part, depth - 2 * part), (0, part), (depth - part, part))
            )]
        return [pltpu.make_async_remote_copy(
            src_ref=fields[step].at[pl.ds(REACH + c * part, part), inner],
            dst_ref=qb[c].at[:, inner],
            send_sem=pair_send.at[c], recv_sem=pair_recv.at[c],
            device_id=partner, device_id_type=MESH,
        ) for c in range(CHUNKS)]

    def forward(ref, index):
        return pltpu.make_async_remote_copy(
            src_ref=ref.at[:, pl.ds(side_from, MARGIN)],
            dst_ref=ref.at[:, pl.ds(side_to, MARGIN)],
            send_sem=fwd_send.at[index], recv_sem=fwd_recv.at[index],
            device_id=peer, device_id_type=MESH,
        )

    def clear(ref, pads):
        rows, width = ref.shape[0], ref.shape[1]

        def body(z, carry):
            ref[z, 0:MARGIN] = jnp.zeros((MARGIN, along), jnp.float32)
            ref[z, width - MARGIN : width] = jnp.zeros((MARGIN, along), jnp.float32)
            return carry

        lax.fori_loop(0, rows, body, 0)
        if pads:
            for z in list(range(REACH)) + list(range(rows - REACH, rows)):
                ref[z, inner] = jnp.zeros((cols, along), jnp.float32)

    for ref in fields:
        clear(ref, ref is not p4)
    for ref in [qa] + qb:
        clear(ref, False)

    barrier = pltpu.get_barrier_semaphore()
    pl.semaphore_signal(barrier, inc=1, device_id=peer, device_id_type=MESH)
    pl.semaphore_signal(barrier, inc=1, device_id=partner, device_id_type=MESH)

    @pl.when(has_low)
    def _():
        pl.semaphore_signal(barrier, inc=1, device_id=low, device_id_type=MESH)

    @pl.when(has_high)
    def _():
        pl.semaphore_signal(barrier, inc=1, device_id=high, device_id_type=MESH)

    pl.semaphore_wait(
        barrier, 2 + jnp.where(has_low, 1, 0) + jnp.where(has_high, 1, 0)
    )

    def start_depth(step):
        @pl.when(has_low)
        def _():
            low_copy(step).start()

        @pl.when(has_high)
        def _():
            high_copy(step).start()

    loads[0].wait()
    start_depth(0)
    side_copy(0).start()

    for load in loads[1:5]:
        load.wait()

    count = cells_ref.shape[1]
    first_lane = lax.broadcasted_iota(jnp.int32, (1, count), 1) == 0
    cells = jnp.where(
        is_receiver, cells_ref[...], jnp.where(first_lane, source_ref[0], -1)
    )
    depth_start = jnp.where(
        is_receiver, lax.rem(slab + quarter, slabs), slab - quarter
    ) * depth
    cols_all = 2 * cols
    safe = jnp.maximum(cells, 0)
    cell_depth = lax.div(safe, cols_all * along) - depth_start
    cell_across = lax.rem(lax.div(safe, along), cols_all) - side * cols
    cell_along = lax.rem(safe, along)
    inside = (
        (cells >= 0) & (cell_depth >= 0) & (cell_depth < depth)
        & (cell_across >= 0) & (cell_across < cols)
    )
    cell_row = jnp.where(inside, cell_depth * cols + cell_across, -1)
    row_hot = jnp.where(
        lax.broadcasted_iota(jnp.int32, (depth * cols, count), 0) == cell_row, 1.0, 0.0
    ).astype(jnp.bfloat16)
    along_hot = lax.broadcasted_iota(jnp.int32, (along, count), 0) == cell_along
    over_cells = (((1,), (1,)), ((), ()))

    def make_impulse(step):
        amount = jnp.where(
            is_receiver,
            traces_ref[step : step + 1, :],
            jnp.where(first_lane, wavelet_ref[step], 0.0),
        )
        spread = jnp.concatenate(split_bf16(jnp.where(along_hot, amount, 0.0)), axis=0)
        both = lax.dot_general(row_hot, spread, over_cells, preferred_element_type=jnp.float32)
        impulse[step] = (both[:, :along] + both[:, along:]).reshape(depth, cols, along)

    make_impulse(0)

    apart = jnp.abs(
        lax.broadcasted_iota(jnp.int32, (along, along), 0)
        - lax.broadcasted_iota(jnp.int32, (along, along), 1)
    )
    band = jnp.where(apart == 0, 3.0 * STENCIL_WEIGHTS[0], 0.0)
    for reach in range(1, REACH + 1):
        band = jnp.where(apart == reach, STENCIL_WEIGHTS[reach], band)
    band_high, band_low = split_bf16(band)

    def advance(step, first):
        field, later = fields[step], fields[step + 1]
        zs = pl.ds(first, part)
        centre = field[pl.ds(first + REACH, part), inner]
        c_high, c_low = split_bf16(centre.reshape(part * cols, along))
        summed = (
            jnp.dot(c_high, band_high, preferred_element_type=jnp.float32)
            + jnp.dot(c_low, band_high, preferred_element_type=jnp.float32)
            + jnp.dot(c_high, band_low, preferred_element_type=jnp.float32)
        ).reshape(part, cols, along)
        for reach in range(1, REACH + 1):
            pairs = (
                field[pl.ds(first + REACH + reach, part), inner]
                + field[pl.ds(first + REACH - reach, part), inner]
            ) + (
                field[pl.ds(first + REACH, part), MARGIN + reach : MARGIN + reach + cols]
                + field[pl.ds(first + REACH, part), MARGIN - reach : MARGIN - reach + cols]
            )
            summed = summed + STENCIL_WEIGHTS[reach] * pairs
        if step == 0:
            before = before_ref[zs]
        else:
            before = fields[step - 1][pl.ds(first + REACH, part), inner]
        result = 2.0 * centre - before + courant_ref[zs] * (summed + impulse[step, zs])
        later[pl.ds(first + REACH, part), inner] = result

    for load in loads[5:]:
        load.wait()
    for step in range(STEPS):
        side_copy(step).wait_recv()

        def body(c, carry, step=step):
            advance(step, c * part)
            return carry

        lax.fori_loop(1, CHUNKS - 1, body, 0)

        sends_pair = is_source if step % 2 else is_receiver
        copies = pair_copies(step + 1, step >= 2)
        if step < 2:
            @pl.when(sends_pair)
            def _():
                copies[0].start()

        @pl.when(has_high)
        def _():
            low_copy(step).wait_recv()

        @pl.when(has_low)
        def _():
            high_copy(step).wait_recv()

        def edge(c, carry, step=step):
            advance(step, c * (depth - part))
            return carry

        lax.fori_loop(0, 2, edge, 0)
        if step < STEPS - 1:
            start_depth(step + 1)
        side_copy(step + 1).start()

        @pl.when(sends_pair)
        def _():
            for copy in copies[1:] if step < 2 else copies:
                copy.start()

        if step == 0:
            for later_step in range(1, STEPS):
                make_impulse(later_step)

    stores = [
        pltpu.make_async_copy(
            ref.at[pl.ds(REACH, depth), inner], target, store_sem.at[CHUNKS + index]
        )
        for index, (ref, target) in enumerate(((p4, now_out), (p3, before_out)))
    ]
    for store in stores:
        store.start()
    side_copy(STEPS).wait_recv()
    for copy in pair_copies(1, False):
        copy.wait_recv()
    forward(qa, CHUNKS).start()
    forward(qa, CHUNKS).wait_recv()
    slot_base = jnp.where(is_receiver, MARGIN, 0)
    sign = jnp.where(is_receiver, 1, -1)

    def starts(slot):
        lag = (offsets_ref[slot_base + slot] - MARGIN) * sign
        return MARGIN + lag, MARGIN - lag

    def first_product(own):
        def body(slot, carry):
            own_at, other_at = starts(slot)
            for z in range(depth):
                partial[z, slot] = (
                    own[REACH + z, pl.ds(own_at, cols)] * qa[z, pl.ds(other_at, cols)]
                )
            return carry

        lax.fori_loop(0, MARGIN, body, 0)

    def last_product(own, c):
        def body(slot, carry):
            own_at, other_at = starts(slot)
            for z in range(part):
                row = c * part + z
                image_ref[row, slot] = (
                    partial[row, slot]
                    + own[REACH + row, pl.ds(own_at, cols)]
                    * qb[c][z, pl.ds(other_at, cols)]
                ).astype(jnp.bfloat16)
            return carry

        lax.fori_loop(0, MARGIN, body, 0)

    @pl.when(is_source)
    def _():
        first_product(p4)

    @pl.when(is_receiver)
    def _():
        first_product(p3)

    seconds = pair_copies(3, True)
    seconds[0].wait_recv()
    forward(qb[0], 0).start()
    for c in range(CHUNKS):
        if c + 1 < CHUNKS:
            seconds[c + 1].wait_recv()
            forward(qb[c + 1], c + 1).start()
        forward(qb[c], c).wait_recv()

        @pl.when(is_source)
        def _():
            last_product(p2, c)

        @pl.when(is_receiver)
        def _():
            last_product(p1, c)

        rows = pl.ds(c * part, part)
        stores.append(
            pltpu.make_async_copy(image_ref.at[rows], image_out.at[rows], store_sem.at[c])
        )
        stores[-1].start()

    for store in stores:
        store.wait()
    for step in range(STEPS):
        @pl.when(has_low)
        def _():
            low_copy(step).wait_send()

        @pl.when(has_high)
        def _():
            high_copy(step).wait_send()

    for step in range(STEPS + 1):
        side_copy(step).wait_send()
    for copy in pair_copies(1, False):
        copy.wait_send()
    for c in range(CHUNKS):
        seconds[c].wait_send()
        forward(qb[c], c).wait_send()
    forward(qa, CHUNKS).wait_send()


def store_kernel(now_in, before_in, image_in, now_out, before_out, image_out, sem):
    depth = now_in.shape[0]
    pieces = []
    for source, target, count in (
        (image_in, image_out, 8), (now_in, now_out, 2), (before_in, before_out, 2),
    ):
        rows = depth // count
        pieces += [
            (source.at[pl.ds(k * rows, rows)], target.at[pl.ds(k * rows, rows)])
            for k in range(count)
        ]
    copies = [
        pltpu.make_async_copy(source, target, sem.at[index])
        for index, (source, target) in enumerate(pieces)
    ]
    for copy in copies:
        copy.start()
    for copy in copies:
        copy.wait()


def shards(field_now, field_before, courant, wavelet, source_cell, traces, receiver_cells, offsets):
    depth, cols, along = field_now.shape
    f32 = jnp.float32
    hbm = pl.BlockSpec(memory_space=pltpu.HBM)
    anywhere = pl.BlockSpec(memory_space=pl.ANY)
    i32 = jnp.int32
    field = pltpu.VMEM((depth + 2 * REACH, cols + 2 * MARGIN, along), f32)
    part = depth // CHUNKS
    dma = pltpu.SemaphoreType.DMA
    results = pl.pallas_call(
        functools.partial(kernel, lax.axis_size("slab")),
        out_shape=(
            jax.ShapeDtypeStruct(field_now.shape, f32),
            jax.ShapeDtypeStruct(field_now.shape, f32),
            jax.ShapeDtypeStruct((depth, MARGIN, cols, along), jnp.bfloat16),
        ),
        in_specs=[hbm] * 8,
        out_specs=(anywhere, anywhere, anywhere),
        scratch_shapes=[field] * 5
        + [pltpu.VMEM((depth, cols + 2 * MARGIN, along), f32)]
        + [pltpu.VMEM((part, cols + 2 * MARGIN, along), f32)] * CHUNKS
        + [
            pltpu.VMEM((STEPS, depth, cols, along), f32),
            pltpu.VMEM((depth, MARGIN, cols, along), f32),
            pltpu.VMEM(field_now.shape, f32), pltpu.VMEM(field_now.shape, f32),
            pltpu.VMEM(traces.shape, f32), pltpu.VMEM((1, receiver_cells.shape[0]), i32),
            pltpu.SMEM(wavelet.shape, f32), pltpu.SMEM(source_cell.shape, i32),
            pltpu.SMEM(offsets.shape, i32), dma((8,)),
            pltpu.VMEM((depth, MARGIN, cols, along), jnp.bfloat16), dma((CHUNKS + 2,)),
            dma((STEPS,)), dma((STEPS,)), dma((STEPS,)), dma((STEPS,)),
            dma((STEPS + 1,)), dma((STEPS + 1,)),
            dma((CHUNKS + 3,)), dma((CHUNKS + 3,)), dma((CHUNKS + 1,)), dma((CHUNKS + 1,)),
        ],
        compiler_params=pltpu.CompilerParams(
            collective_id=0, has_side_effects=True, vmem_limit_bytes=61 * 1024 * 1024
        ),
    )(
        field_now, field_before, courant, traces, receiver_cells.reshape(1, -1),
        wavelet, source_cell, offsets,
    )
    return pl.pallas_call(
        store_kernel,
        out_shape=tuple(jax.ShapeDtypeStruct(r.shape, r.dtype) for r in results),
        in_specs=[anywhere] * 3,
        out_specs=(hbm, hbm, hbm),
        scratch_shapes=[dma((12,))],
        compiler_params=pltpu.CompilerParams(vmem_limit_bytes=61 * 1024 * 1024),
    )(*results)


def solution(mesh):
    return jax.shard_map(
        shards,
        mesh=mesh,
        in_specs=(
            P(("shot", "slab"), "side", None),
            P(("shot", "slab"), "side", None),
            P(("shot", "slab"), "side", None),
            P("shot"),
            P("shot"),
            P("shot", None),
            P("shot"),
            P("shot"),
        ),
        out_specs=(
            P(("shot", "slab"), "side", None),
            P(("shot", "slab"), "side", None),
            P(("shot", "slab"), None, "side", None),
        ),
        check_vma=False,
    )
```

```python
import functools

import jax
import jax.numpy as jnp
from jax import lax
from jax.experimental import pallas as pl
from jax.experimental.pallas import tpu as pltpu
from jax.sharding import PartitionSpec as P

LAGS = 32
STEPS = 4
MARGIN = LAGS // 2
REACH = 4
CHUNKS = 4
STENCIL_WEIGHTS = (-205.0 / 72.0, 8.0 / 5.0, -1.0 / 5.0, 8.0 / 315.0, -1.0 / 560.0)
MESH = pl.DeviceIdType.MESH


def split_bf16(value):
    high = value.astype(jnp.bfloat16)
    low = (value - high.astype(jnp.float32)).astype(jnp.bfloat16)
    return high, low


def kernel(
    slabs,
    now_hbm, before_hbm, courant_hbm, traces_hbm, cells_hbm, wavelet_hbm, source_hbm, offsets_hbm,
    now_out, before_out, image_out,
    p0, p1, p2, p3, p4, qa, qb0, qb1, qb2, qb3, impulse, partial,
    before_ref, courant_ref, traces_ref, cells_ref, wavelet_ref, source_ref, offsets_ref, load_sem,
    image_ref, store_sem,
    low_send, low_recv, high_send, high_recv, side_send, side_recv,
    pair_send, pair_recv, fwd_send, fwd_recv,
):
    depth, cols, along = now_hbm.shape
    fields = [p0, p1, p2, p3, p4]
    qb = [qb0, qb1, qb2, qb3]
    part = depth // CHUNKS
    inner = pl.ds(MARGIN, cols)
    shot = lax.axis_index("shot")
    slab = lax.axis_index("slab")
    side = lax.axis_index("side")
    quarter = slabs // 4
    is_receiver = (slab < quarter) | (slab >= 3 * quarter)
    is_source = jnp.logical_not(is_receiver)
    has_low = (slab != quarter) & (slab != 3 * quarter)
    has_high = (slab != quarter - 1) & (slab != 3 * quarter - 1)
    low = (shot, lax.rem(slab + slabs - 1, slabs), side)
    high = (shot, lax.rem(slab + 1, slabs), side)
    partner = (shot, lax.rem(slab + 2 * quarter, slabs), side)
    peer = (shot, slab, 1 - side)

    loads = [
        pltpu.make_async_copy(source, target, load_sem.at[index])
        for index, (source, target) in enumerate((
            (now_hbm, p0.at[pl.ds(REACH, depth), inner]),
            (cells_hbm, cells_ref), (traces_hbm, traces_ref),
            (wavelet_hbm, wavelet_ref), (source_hbm, source_ref),
            (before_hbm, before_ref), (courant_hbm, courant_ref), (offsets_hbm, offsets_ref),
        ))
    ]
    for load in loads:
        load.start()

    def low_copy(step):
        return pltpu.make_async_remote_copy(
            src_ref=fields[step].at[pl.ds(REACH, REACH), inner],
            dst_ref=fields[step].at[pl.ds(REACH + depth, REACH), inner],
            send_sem=low_send.at[step], recv_sem=low_recv.at[step],
            device_id=low, device_id_type=MESH,
        )

    def high_copy(step):
        return pltpu.make_async_remote_copy(
            src_ref=fields[step].at[pl.ds(depth, REACH), inner],
            dst_ref=fields[step].at[pl.ds(0, REACH), inner],
            send_sem=high_send.at[step], recv_sem=high_recv.at[step],
            device_id=high, device_id_type=MESH,
        )

    side_from = pl.multiple_of(jnp.where(side == 0, cols, MARGIN), 8)
    side_to = pl.multiple_of(jnp.where(side == 0, 0, MARGIN + cols), 8)

    def side_copy(step):
        rows = pl.ds(REACH, depth)
        return pltpu.make_async_remote_copy(
            src_ref=fields[step].at[rows, pl.ds(side_from, MARGIN)],
            dst_ref=fields[step].at[rows, pl.ds(side_to, MARGIN)],
            send_sem=side_send.at[step], recv_sem=side_recv.at[step],
            device_id=peer, device_id_type=MESH,
        )

    def pair_copies(step, second):
        if not second:
            return [pltpu.make_async_remote_copy(
                src_ref=fields[step].at[pl.ds(REACH + first, rows), inner],
                dst_ref=qa.at[pl.ds(first, rows), inner],
                send_sem=pair_send.at[CHUNKS + index], recv_sem=pair_recv.at[CHUNKS + index],
                device_id=partner, device_id_type=MESH,
            ) for index, (first, rows) in enumerate(
                ((part, depth - 2 * part), (0, part), (depth - part, part))
            )]
        return [pltpu.make_async_remote_copy(
            src_ref=fields[step].at[pl.ds(REACH + c * part, part), inner],
            dst_ref=qb[c].at[:, inner],
            send_sem=pair_send.at[c], recv_sem=pair_recv.at[c],
            device_id=partner, device_id_type=MESH,
        ) for c in range(CHUNKS)]

    def forward(ref, index):
        return pltpu.make_async_remote_copy(
            src_ref=ref.at[:, pl.ds(side_from, MARGIN)],
            dst_ref=ref.at[:, pl.ds(side_to, MARGIN)],
            send_sem=fwd_send.at[index], recv_sem=fwd_recv.at[index],
            device_id=peer, device_id_type=MESH,
        )

    def clear(ref, pads):
        rows, width = ref.shape[0], ref.shape[1]

        def body(z, carry):
            ref[z, 0:MARGIN] = jnp.zeros((MARGIN, along), jnp.float32)
            ref[z, width - MARGIN : width] = jnp.zeros((MARGIN, along), jnp.float32)
            return carry

        lax.fori_loop(0, rows, body, 0)
        if pads:
            for z in list(range(REACH)) + list(range(rows - REACH, rows)):
                ref[z, inner] = jnp.zeros((cols, along), jnp.float32)

    for ref in fields:
        clear(ref, ref is not p4)
    for ref in [qa] + qb:
        clear(ref, False)

    barrier = pltpu.get_barrier_semaphore()
    pl.semaphore_signal(barrier, inc=1, device_id=peer, device_id_type=MESH)
    pl.semaphore_signal(barrier, inc=1, device_id=partner, device_id_type=MESH)

    @pl.when(has_low)
    def _():
        pl.semaphore_signal(barrier, inc=1, device_id=low, device_id_type=MESH)

    @pl.when(has_high)
    def _():
        pl.semaphore_signal(barrier, inc=1, device_id=high, device_id_type=MESH)

    pl.semaphore_wait(
        barrier, 2 + jnp.where(has_low, 1, 0) + jnp.where(has_high, 1, 0)
    )

    def start_depth(step):
        @pl.when(has_low)
        def _():
            low_copy(step).start()

        @pl.when(has_high)
        def _():
            high_copy(step).start()

    loads[0].wait()
    start_depth(0)
    side_copy(0).start()

    for load in loads[1:5]:
        load.wait()

    count = cells_ref.shape[1]
    first_lane = lax.broadcasted_iota(jnp.int32, (1, count), 1) == 0
    cells = jnp.where(
        is_receiver, cells_ref[...], jnp.where(first_lane, source_ref[0], -1)
    )
    depth_start = jnp.where(
        is_receiver, lax.rem(slab + quarter, slabs), slab - quarter
    ) * depth
    cols_all = 2 * cols
    safe = jnp.maximum(cells, 0)
    cell_depth = lax.div(safe, cols_all * along) - depth_start
    cell_across = lax.rem(lax.div(safe, along), cols_all) - side * cols
    cell_along = lax.rem(safe, along)
    inside = (
        (cells >= 0) & (cell_depth >= 0) & (cell_depth < depth)
        & (cell_across >= 0) & (cell_across < cols)
    )
    cell_row = jnp.where(inside, cell_depth * cols + cell_across, -1)
    row_hot = jnp.where(
        lax.broadcasted_iota(jnp.int32, (depth * cols, count), 0) == cell_row, 1.0, 0.0
    ).astype(jnp.bfloat16)
    along_hot = lax.broadcasted_iota(jnp.int32, (along, count), 0) == cell_along
    over_cells = (((1,), (1,)), ((), ()))

    def make_impulse(step):
        amount = jnp.where(
            is_receiver,
            traces_ref[step : step + 1, :],
            jnp.where(first_lane, wavelet_ref[step], 0.0),
        )
        spread = jnp.concatenate(split_bf16(jnp.where(along_hot, amount, 0.0)), axis=0)
        both = lax.dot_general(row_hot, spread, over_cells, preferred_element_type=jnp.float32)
        impulse[step] = (both[:, :along] + both[:, along:]).reshape(depth, cols, along)

    make_impulse(0)

    apart = jnp.abs(
        lax.broadcasted_iota(jnp.int32, (along, along), 0)
        - lax.broadcasted_iota(jnp.int32, (along, along), 1)
    )
    band = jnp.where(apart == 0, 3.0 * STENCIL_WEIGHTS[0], 0.0)
    for reach in range(1, REACH + 1):
        band = jnp.where(apart == reach, STENCIL_WEIGHTS[reach], band)
    band_high, band_low = split_bf16(band)

    def advance(step, first):
        field, later = fields[step], fields[step + 1]
        zs = pl.ds(first, part)
        centre = field[pl.ds(first + REACH, part), inner]
        c_high, c_low = split_bf16(centre.reshape(part * cols, along))
        summed = (
            jnp.dot(c_high, band_high, preferred_element_type=jnp.float32)
            + jnp.dot(c_low, band_high, preferred_element_type=jnp.float32)
            + jnp.dot(c_high, band_low, preferred_element_type=jnp.float32)
        ).reshape(part, cols, along)
        for reach in range(1, REACH + 1):
            pairs = (
                field[pl.ds(first + REACH + reach, part), inner]
                + field[pl.ds(first + REACH - reach, part), inner]
            ) + (
                field[pl.ds(first + REACH, part), MARGIN + reach : MARGIN + reach + cols]
                + field[pl.ds(first + REACH, part), MARGIN - reach : MARGIN - reach + cols]
            )
            summed = summed + STENCIL_WEIGHTS[reach] * pairs
        if step == 0:
            before = before_ref[zs]
        else:
            before = fields[step - 1][pl.ds(first + REACH, part), inner]
        result = 2.0 * centre - before + courant_ref[zs] * (summed + impulse[step, zs])
        later[pl.ds(first + REACH, part), inner] = result

    for load in loads[5:]:
        load.wait()
    for step in range(STEPS):
        side_copy(step).wait_recv()

        def body(c, carry, step=step):
            advance(step, c * part)
            return carry

        lax.fori_loop(1, CHUNKS - 1, body, 0)

        sends_pair = is_source if step % 2 else is_receiver
        copies = pair_copies(step + 1, step >= 2)
        if step < 2:
            @pl.when(sends_pair)
            def _():
                copies[0].start()

        @pl.when(has_high)
        def _():
            low_copy(step).wait_recv()

        @pl.when(has_low)
        def _():
            high_copy(step).wait_recv()

        def edge(c, carry, step=step):
            advance(step, c * (depth - part))
            return carry

        lax.fori_loop(0, 2, edge, 0)
        if step < STEPS - 1:
            start_depth(step + 1)
        side_copy(step + 1).start()

        @pl.when(sends_pair)
        def _():
            for copy in copies[1:] if step < 2 else copies:
                copy.start()

        if step == 0:
            for later_step in range(1, STEPS):
                make_impulse(later_step)

    stores = [
        pltpu.make_async_copy(
            ref.at[pl.ds(REACH, depth), inner], target, store_sem.at[CHUNKS + index]
        )
        for index, (ref, target) in enumerate(((p4, now_out), (p3, before_out)))
    ]
    for store in stores:
        store.start()
    side_copy(STEPS).wait_recv()
    for copy in pair_copies(1, False):
        copy.wait_recv()
    forward(qa, CHUNKS).start()
    forward(qa, CHUNKS).wait_recv()
    slot_base = jnp.where(is_receiver, MARGIN, 0)
    sign = jnp.where(is_receiver, 1, -1)

    def starts(slot):
        lag = (offsets_ref[slot_base + slot] - MARGIN) * sign
        return MARGIN + lag, MARGIN - lag

    def first_product(own):
        def body(slot, carry):
            own_at, other_at = starts(slot)
            for z in range(depth):
                partial[z, slot] = (
                    own[REACH + z, pl.ds(own_at, cols)] * qa[z, pl.ds(other_at, cols)]
                )
            return carry

        lax.fori_loop(0, MARGIN, body, 0)

    def last_product(own, c):
        def body(slot, carry):
            own_at, other_at = starts(slot)
            for z in range(part):
                row = c * part + z
                image_ref[row, slot] = (
                    partial[row, slot]
                    + own[REACH + row, pl.ds(own_at, cols)]
                    * qb[c][z, pl.ds(other_at, cols)]
                ).astype(jnp.bfloat16)
            return carry

        lax.fori_loop(0, MARGIN, body, 0)

    @pl.when(is_source)
    def _():
        first_product(p4)

    @pl.when(is_receiver)
    def _():
        first_product(p3)

    seconds = pair_copies(3, True)
    seconds[0].wait_recv()
    forward(qb[0], 0).start()
    for c in range(CHUNKS):
        if c + 1 < CHUNKS:
            seconds[c + 1].wait_recv()
            forward(qb[c + 1], c + 1).start()
        forward(qb[c], c).wait_recv()

        @pl.when(is_source)
        def _():
            last_product(p2, c)

        @pl.when(is_receiver)
        def _():
            last_product(p1, c)

        rows = pl.ds(c * part, part)
        stores.append(
            pltpu.make_async_copy(image_ref.at[rows], image_out.at[rows], store_sem.at[c])
        )
        stores[-1].start()

    for store in stores:
        store.wait()
    for step in range(STEPS):
        @pl.when(has_low)
        def _():
            low_copy(step).wait_send()

        @pl.when(has_high)
        def _():
            high_copy(step).wait_send()

    for step in range(STEPS + 1):
        side_copy(step).wait_send()
    for copy in pair_copies(1, False):
        copy.wait_send()
    for c in range(CHUNKS):
        seconds[c].wait_send()
        forward(qb[c], c).wait_send()
    forward(qa, CHUNKS).wait_send()


def store_kernel(
    now_in, before_in, image_in, now_out, before_out, image_out,
    now_held, before_held, image_held, in_sem, out_sem,
):
    depth = now_in.shape[0]
    fetches, stores = [], []
    for source, held, target, count in (
        (image_in, image_held, image_out, 4),
        (now_in, now_held, now_out, 1),
        (before_in, before_held, before_out, 1),
    ):
        rows = depth // count
        for k in range(count):
            piece = pl.ds(k * rows, rows)
            index = len(fetches)
            fetches.append(
                pltpu.make_async_copy(source.at[piece], held.at[piece], in_sem.at[index])
            )
            stores.append(
                pltpu.make_async_copy(held.at[piece], target.at[piece], out_sem.at[index])
            )
    for fetch in fetches:
        fetch.start()
    for fetch, store in zip(fetches, stores):
        fetch.wait()
        store.start()
    for store in stores:
        store.wait()


def shards(field_now, field_before, courant, wavelet, source_cell, traces, receiver_cells, offsets):
    depth, cols, along = field_now.shape
    f32 = jnp.float32
    hbm = pl.BlockSpec(memory_space=pltpu.HBM)
    anywhere = pl.BlockSpec(memory_space=pl.ANY)
    i32 = jnp.int32
    field = pltpu.VMEM((depth + 2 * REACH, cols + 2 * MARGIN, along), f32)
    part = depth // CHUNKS
    dma = pltpu.SemaphoreType.DMA
    results = pl.pallas_call(
        functools.partial(kernel, lax.axis_size("slab")),
        out_shape=(
            jax.ShapeDtypeStruct(field_now.shape, f32),
            jax.ShapeDtypeStruct(field_now.shape, f32),
            jax.ShapeDtypeStruct((depth, MARGIN, cols, along), jnp.bfloat16),
        ),
        in_specs=[hbm] * 8,
        out_specs=(anywhere, anywhere, anywhere),
        scratch_shapes=[field] * 5
        + [pltpu.VMEM((depth, cols + 2 * MARGIN, along), f32)]
        + [pltpu.VMEM((part, cols + 2 * MARGIN, along), f32)] * CHUNKS
        + [
            pltpu.VMEM((STEPS, depth, cols, along), f32),
            pltpu.VMEM((depth, MARGIN, cols, along), f32),
            pltpu.VMEM(field_now.shape, f32), pltpu.VMEM(field_now.shape, f32),
            pltpu.VMEM(traces.shape, f32), pltpu.VMEM((1, receiver_cells.shape[0]), i32),
            pltpu.SMEM(wavelet.shape, f32), pltpu.SMEM(source_cell.shape, i32),
            pltpu.SMEM(offsets.shape, i32), dma((8,)),
            pltpu.VMEM((depth, MARGIN, cols, along), jnp.bfloat16), dma((CHUNKS + 2,)),
            dma((STEPS,)), dma((STEPS,)), dma((STEPS,)), dma((STEPS,)),
            dma((STEPS + 1,)), dma((STEPS + 1,)),
            dma((CHUNKS + 3,)), dma((CHUNKS + 3,)), dma((CHUNKS + 1,)), dma((CHUNKS + 1,)),
        ],
        compiler_params=pltpu.CompilerParams(
            collective_id=0, has_side_effects=True, vmem_limit_bytes=61 * 1024 * 1024
        ),
    )(
        field_now, field_before, courant, traces, receiver_cells.reshape(1, -1),
        wavelet, source_cell, offsets,
    )
    return pl.pallas_call(
        store_kernel,
        out_shape=tuple(jax.ShapeDtypeStruct(r.shape, r.dtype) for r in results),
        in_specs=[anywhere] * 3,
        out_specs=(hbm, hbm, hbm),
        scratch_shapes=[pltpu.VMEM(r.shape, r.dtype) for r in results] + [dma((6,)), dma((6,))],
        compiler_params=pltpu.CompilerParams(vmem_limit_bytes=61 * 1024 * 1024),
    )(*results)


def solution(mesh):
    return jax.shard_map(
        shards,
        mesh=mesh,
        in_specs=(
            P(("shot", "slab"), "side", None),
            P(("shot", "slab"), "side", None),
            P(("shot", "slab"), "side", None),
            P("shot"),
            P("shot"),
            P("shot", None),
            P("shot"),
            P("shot"),
        ),
        out_specs=(
            P(("shot", "slab"), "side", None),
            P(("shot", "slab"), "side", None),
            P(("shot", "slab"), None, "side", None),
        ),
        check_vma=False,
    )
```

```python
import functools

import jax
import jax.numpy as jnp
from jax import lax
from jax.experimental import pallas as pl
from jax.experimental.pallas import tpu as pltpu
from jax.sharding import PartitionSpec as P

LAGS = 32
STEPS = 4
MARGIN = LAGS // 2
REACH = 4
CHUNKS = 4
STENCIL_WEIGHTS = (-205.0 / 72.0, 8.0 / 5.0, -1.0 / 5.0, 8.0 / 315.0, -1.0 / 560.0)
MESH = pl.DeviceIdType.MESH


def split_bf16(value):
    high = value.astype(jnp.bfloat16)
    low = (value - high.astype(jnp.float32)).astype(jnp.bfloat16)
    return high, low


def kernel(
    slabs,
    now_hbm, before_hbm, courant_hbm, traces_hbm, cells_hbm, wavelet_hbm, source_hbm, offsets_hbm,
    now_out, before_out, image_out,
    p0, p1, p2, p3, p4, qa, qb0, qb1, qb2, qb3, impulse, partial,
    before_ref, courant_ref, traces_ref, cells_ref, wavelet_ref, source_ref, offsets_ref, load_sem,
    image_ref, store_sem,
    low_send, low_recv, high_send, high_recv, side_send, side_recv,
    pair_send, pair_recv, fwd_send, fwd_recv,
):
    depth, cols, along = now_hbm.shape
    fields = [p0, p1, p2, p3, p4]
    qb = [qb0, qb1, qb2, qb3]
    part = depth // CHUNKS
    inner = pl.ds(MARGIN, cols)
    shot = lax.axis_index("shot")
    slab = lax.axis_index("slab")
    side = lax.axis_index("side")
    quarter = slabs // 4
    is_receiver = (slab < quarter) | (slab >= 3 * quarter)
    is_source = jnp.logical_not(is_receiver)
    has_low = (slab != quarter) & (slab != 3 * quarter)
    has_high = (slab != quarter - 1) & (slab != 3 * quarter - 1)
    low = (shot, lax.rem(slab + slabs - 1, slabs), side)
    high = (shot, lax.rem(slab + 1, slabs), side)
    partner = (shot, lax.rem(slab + 2 * quarter, slabs), side)
    peer = (shot, slab, 1 - side)

    loads = [
        pltpu.make_async_copy(source, target, load_sem.at[index])
        for index, (source, target) in enumerate((
            (now_hbm, p0.at[pl.ds(REACH, depth), inner]),
            (cells_hbm, cells_ref), (traces_hbm, traces_ref),
            (wavelet_hbm, wavelet_ref), (source_hbm, source_ref),
            (before_hbm, before_ref), (courant_hbm, courant_ref), (offsets_hbm, offsets_ref),
        ))
    ]
    for load in loads:
        load.start()

    def low_copy(step):
        return pltpu.make_async_remote_copy(
            src_ref=fields[step].at[pl.ds(REACH, REACH), inner],
            dst_ref=fields[step].at[pl.ds(REACH + depth, REACH), inner],
            send_sem=low_send.at[step], recv_sem=low_recv.at[step],
            device_id=low, device_id_type=MESH,
        )

    def high_copy(step):
        return pltpu.make_async_remote_copy(
            src_ref=fields[step].at[pl.ds(depth, REACH), inner],
            dst_ref=fields[step].at[pl.ds(0, REACH), inner],
            send_sem=high_send.at[step], recv_sem=high_recv.at[step],
            device_id=high, device_id_type=MESH,
        )

    side_from = pl.multiple_of(jnp.where(side == 0, cols, MARGIN), 8)
    side_to = pl.multiple_of(jnp.where(side == 0, 0, MARGIN + cols), 8)

    def side_copy(step):
        rows = pl.ds(REACH, depth)
        return pltpu.make_async_remote_copy(
            src_ref=fields[step].at[rows, pl.ds(side_from, MARGIN)],
            dst_ref=fields[step].at[rows, pl.ds(side_to, MARGIN)],
            send_sem=side_send.at[step], recv_sem=side_recv.at[step],
            device_id=peer, device_id_type=MESH,
        )

    def pair_copies(step, second):
        if not second:
            return [pltpu.make_async_remote_copy(
                src_ref=fields[step].at[pl.ds(REACH + first, rows), inner],
                dst_ref=qa.at[pl.ds(first, rows), inner],
                send_sem=pair_send.at[CHUNKS + index], recv_sem=pair_recv.at[CHUNKS + index],
                device_id=partner, device_id_type=MESH,
            ) for index, (first, rows) in enumerate(
                ((part, depth - 2 * part), (0, part), (depth - part, part))
            )]
        return [pltpu.make_async_remote_copy(
            src_ref=fields[step].at[pl.ds(REACH + c * part, part), inner],
            dst_ref=qb[c].at[:, inner],
            send_sem=pair_send.at[c], recv_sem=pair_recv.at[c],
            device_id=partner, device_id_type=MESH,
        ) for c in range(CHUNKS)]

    def forward(ref, index):
        return pltpu.make_async_remote_copy(
            src_ref=ref.at[:, pl.ds(side_from, MARGIN)],
            dst_ref=ref.at[:, pl.ds(side_to, MARGIN)],
            send_sem=fwd_send.at[index], recv_sem=fwd_recv.at[index],
            device_id=peer, device_id_type=MESH,
        )

    def clear(ref, pads):
        rows, width = ref.shape[0], ref.shape[1]

        def body(z, carry):
            ref[z, 0:MARGIN] = jnp.zeros((MARGIN, along), jnp.float32)
            ref[z, width - MARGIN : width] = jnp.zeros((MARGIN, along), jnp.float32)
            return carry

        lax.fori_loop(0, rows, body, 0)
        if pads:
            for z in list(range(REACH)) + list(range(rows - REACH, rows)):
                ref[z, inner] = jnp.zeros((cols, along), jnp.float32)

    for ref in fields:
        clear(ref, ref is not p4)
    for ref in [qa] + qb:
        clear(ref, False)

    barrier = pltpu.get_barrier_semaphore()
    pl.semaphore_signal(barrier, inc=1, device_id=peer, device_id_type=MESH)
    pl.semaphore_signal(barrier, inc=1, device_id=partner, device_id_type=MESH)

    @pl.when(has_low)
    def _():
        pl.semaphore_signal(barrier, inc=1, device_id=low, device_id_type=MESH)

    @pl.when(has_high)
    def _():
        pl.semaphore_signal(barrier, inc=1, device_id=high, device_id_type=MESH)

    pl.semaphore_wait(
        barrier, 2 + jnp.where(has_low, 1, 0) + jnp.where(has_high, 1, 0)
    )

    def start_depth(step):
        @pl.when(has_low)
        def _():
            low_copy(step).start()

        @pl.when(has_high)
        def _():
            high_copy(step).start()

    loads[0].wait()
    start_depth(0)
    side_copy(0).start()

    for load in loads[1:5]:
        load.wait()

    count = cells_ref.shape[1]
    first_lane = lax.broadcasted_iota(jnp.int32, (1, count), 1) == 0
    cells = jnp.where(
        is_receiver, cells_ref[...], jnp.where(first_lane, source_ref[0], -1)
    )
    depth_start = jnp.where(
        is_receiver, lax.rem(slab + quarter, slabs), slab - quarter
    ) * depth
    cols_all = 2 * cols
    safe = jnp.maximum(cells, 0)
    cell_depth = lax.div(safe, cols_all * along) - depth_start
    cell_across = lax.rem(lax.div(safe, along), cols_all) - side * cols
    cell_along = lax.rem(safe, along)
    inside = (
        (cells >= 0) & (cell_depth >= 0) & (cell_depth < depth)
        & (cell_across >= 0) & (cell_across < cols)
    )
    cell_row = jnp.where(inside, cell_depth * cols + cell_across, -1)
    row_hot = jnp.where(
        lax.broadcasted_iota(jnp.int32, (depth * cols, count), 0) == cell_row, 1.0, 0.0
    ).astype(jnp.bfloat16)
    along_hot = lax.broadcasted_iota(jnp.int32, (along, count), 0) == cell_along
    over_cells = (((1,), (1,)), ((), ()))

    def make_impulse(step):
        amount = jnp.where(
            is_receiver,
            traces_ref[step : step + 1, :],
            jnp.where(first_lane, wavelet_ref[step], 0.0),
        )
        spread = jnp.concatenate(split_bf16(jnp.where(along_hot, amount, 0.0)), axis=0)
        both = lax.dot_general(row_hot, spread, over_cells, preferred_element_type=jnp.float32)
        impulse[step] = (both[:, :along] + both[:, along:]).reshape(depth, cols, along)

    make_impulse(0)

    apart = jnp.abs(
        lax.broadcasted_iota(jnp.int32, (along, along), 0)
        - lax.broadcasted_iota(jnp.int32, (along, along), 1)
    )
    band = jnp.where(apart == 0, 3.0 * STENCIL_WEIGHTS[0], 0.0)
    for reach in range(1, REACH + 1):
        band = jnp.where(apart == reach, STENCIL_WEIGHTS[reach], band)
    band_high, band_low = split_bf16(band)

    def advance(step, first):
        field, later = fields[step], fields[step + 1]
        zs = pl.ds(first, part)
        centre = field[pl.ds(first + REACH, part), inner]
        c_high, c_low = split_bf16(centre.reshape(part * cols, along))
        summed = (
            jnp.dot(c_high, band_high, preferred_element_type=jnp.float32)
            + jnp.dot(c_low, band_high, preferred_element_type=jnp.float32)
            + jnp.dot(c_high, band_low, preferred_element_type=jnp.float32)
        ).reshape(part, cols, along)
        for reach in range(1, REACH + 1):
            pairs = (
                field[pl.ds(first + REACH + reach, part), inner]
                + field[pl.ds(first + REACH - reach, part), inner]
            ) + (
                field[pl.ds(first + REACH, part), MARGIN + reach : MARGIN + reach + cols]
                + field[pl.ds(first + REACH, part), MARGIN - reach : MARGIN - reach + cols]
            )
            summed = summed + STENCIL_WEIGHTS[reach] * pairs
        if step == 0:
            before = before_ref[zs]
        else:
            before = fields[step - 1][pl.ds(first + REACH, part), inner]
        result = 2.0 * centre - before + courant_ref[zs] * (summed + impulse[step, zs])
        later[pl.ds(first + REACH, part), inner] = result

    for load in loads[5:]:
        load.wait()
    for step in range(STEPS):
        side_copy(step).wait_recv()

        def body(c, carry, step=step):
            advance(step, c * part)
            return carry

        lax.fori_loop(1, CHUNKS - 1, body, 0)

        sends_pair = is_source if step % 2 else is_receiver
        copies = pair_copies(step + 1, step >= 2)
        early = copies[:1] if step < 2 else copies[1:-1]
        late = copies[1:] if step < 2 else [copies[0], copies[-1]]

        @pl.when(sends_pair)
        def _():
            for copy in early:
                copy.start()

        @pl.when(has_high)
        def _():
            low_copy(step).wait_recv()

        @pl.when(has_low)
        def _():
            high_copy(step).wait_recv()

        def edge(c, carry, step=step):
            advance(step, c * (depth - part))
            return carry

        lax.fori_loop(0, 2, edge, 0)
        if step < STEPS - 1:
            start_depth(step + 1)
        side_copy(step + 1).start()

        @pl.when(sends_pair)
        def _():
            for copy in late:
                copy.start()

        if step == 0:
            for later_step in range(1, STEPS):
                make_impulse(later_step)

    stores = [
        pltpu.make_async_copy(
            ref.at[pl.ds(REACH, depth), inner], target, store_sem.at[CHUNKS + index]
        )
        for index, (ref, target) in enumerate(((p4, now_out), (p3, before_out)))
    ]
    for store in stores:
        store.start()
    side_copy(STEPS).wait_recv()
    for copy in pair_copies(1, False):
        copy.wait_recv()
    forward(qa, CHUNKS).start()
    forward(qa, CHUNKS).wait_recv()
    slot_base = jnp.where(is_receiver, MARGIN, 0)
    sign = jnp.where(is_receiver, 1, -1)

    def starts(slot):
        lag = (offsets_ref[slot_base + slot] - MARGIN) * sign
        return MARGIN + lag, MARGIN - lag

    def first_product(own):
        def body(slot, carry):
            own_at, other_at = starts(slot)
            for z in range(depth):
                partial[z, slot] = (
                    own[REACH + z, pl.ds(own_at, cols)] * qa[z, pl.ds(other_at, cols)]
                )
            return carry

        lax.fori_loop(0, MARGIN, body, 0)

    def last_product(own, c):
        def body(slot, carry):
            own_at, other_at = starts(slot)
            for z in range(part):
                row = c * part + z
                image_ref[row, slot] = (
                    partial[row, slot]
                    + own[REACH + row, pl.ds(own_at, cols)]
                    * qb[c][z, pl.ds(other_at, cols)]
                ).astype(jnp.bfloat16)
            return carry

        lax.fori_loop(0, MARGIN, body, 0)

    @pl.when(is_source)
    def _():
        first_product(p4)

    @pl.when(is_receiver)
    def _():
        first_product(p3)

    seconds = pair_copies(3, True)
    order = list(range(1, CHUNKS - 1)) + [0, CHUNKS - 1]
    seconds[order[0]].wait_recv()
    forward(qb[order[0]], order[0]).start()
    for place, c in enumerate(order):
        if place + 1 < CHUNKS:
            after = order[place + 1]
            seconds[after].wait_recv()
            forward(qb[after], after).start()
        forward(qb[c], c).wait_recv()

        @pl.when(is_source)
        def _():
            last_product(p2, c)

        @pl.when(is_receiver)
        def _():
            last_product(p1, c)

        rows = pl.ds(c * part, part)
        stores.append(
            pltpu.make_async_copy(image_ref.at[rows], image_out.at[rows], store_sem.at[c])
        )
        stores[-1].start()

    for store in stores:
        store.wait()
    for step in range(STEPS):
        @pl.when(has_low)
        def _():
            low_copy(step).wait_send()

        @pl.when(has_high)
        def _():
            high_copy(step).wait_send()

    for step in range(STEPS + 1):
        side_copy(step).wait_send()
    for copy in pair_copies(1, False):
        copy.wait_send()
    for c in range(CHUNKS):
        seconds[c].wait_send()
        forward(qb[c], c).wait_send()
    forward(qa, CHUNKS).wait_send()


def store_kernel(
    now_in, before_in, image_in, now_out, before_out, image_out,
    now_held, before_held, image_held, in_sem, out_sem,
):
    depth = now_in.shape[0]
    fetches, stores = [], []
    for source, held, target, count in (
        (image_in, image_held, image_out, 4),
        (now_in, now_held, now_out, 1),
        (before_in, before_held, before_out, 1),
    ):
        rows = depth // count
        for k in range(count):
            piece = pl.ds(k * rows, rows)
            index = len(fetches)
            fetches.append(
                pltpu.make_async_copy(source.at[piece], held.at[piece], in_sem.at[index])
            )
            stores.append(
                pltpu.make_async_copy(held.at[piece], target.at[piece], out_sem.at[index])
            )
    for fetch in fetches:
        fetch.start()
    for fetch, store in zip(fetches, stores):
        fetch.wait()
        store.start()
    for store in stores:
        store.wait()


def shards(field_now, field_before, courant, wavelet, source_cell, traces, receiver_cells, offsets):
    depth, cols, along = field_now.shape
    f32 = jnp.float32
    hbm = pl.BlockSpec(memory_space=pltpu.HBM)
    anywhere = pl.BlockSpec(memory_space=pl.ANY)
    i32 = jnp.int32
    field = pltpu.VMEM((depth + 2 * REACH, cols + 2 * MARGIN, along), f32)
    part = depth // CHUNKS
    dma = pltpu.SemaphoreType.DMA
    results = pl.pallas_call(
        functools.partial(kernel, lax.axis_size("slab")),
        out_shape=(
            jax.ShapeDtypeStruct(field_now.shape, f32),
            jax.ShapeDtypeStruct(field_now.shape, f32),
            jax.ShapeDtypeStruct((depth, MARGIN, cols, along), jnp.bfloat16),
        ),
        in_specs=[hbm] * 8,
        out_specs=(anywhere, anywhere, anywhere),
        scratch_shapes=[field] * 5
        + [pltpu.VMEM((depth, cols + 2 * MARGIN, along), f32)]
        + [pltpu.VMEM((part, cols + 2 * MARGIN, along), f32)] * CHUNKS
        + [
            pltpu.VMEM((STEPS, depth, cols, along), f32),
            pltpu.VMEM((depth, MARGIN, cols, along), f32),
            pltpu.VMEM(field_now.shape, f32), pltpu.VMEM(field_now.shape, f32),
            pltpu.VMEM(traces.shape, f32), pltpu.VMEM((1, receiver_cells.shape[0]), i32),
            pltpu.SMEM(wavelet.shape, f32), pltpu.SMEM(source_cell.shape, i32),
            pltpu.SMEM(offsets.shape, i32), dma((8,)),
            pltpu.VMEM((depth, MARGIN, cols, along), jnp.bfloat16), dma((CHUNKS + 2,)),
            dma((STEPS,)), dma((STEPS,)), dma((STEPS,)), dma((STEPS,)),
            dma((STEPS + 1,)), dma((STEPS + 1,)),
            dma((CHUNKS + 3,)), dma((CHUNKS + 3,)), dma((CHUNKS + 1,)), dma((CHUNKS + 1,)),
        ],
        compiler_params=pltpu.CompilerParams(
            collective_id=0, has_side_effects=True, vmem_limit_bytes=61 * 1024 * 1024
        ),
    )(
        field_now, field_before, courant, traces, receiver_cells.reshape(1, -1),
        wavelet, source_cell, offsets,
    )
    return pl.pallas_call(
        store_kernel,
        out_shape=tuple(jax.ShapeDtypeStruct(r.shape, r.dtype) for r in results),
        in_specs=[anywhere] * 3,
        out_specs=(hbm, hbm, hbm),
        scratch_shapes=[pltpu.VMEM(r.shape, r.dtype) for r in results] + [dma((6,)), dma((6,))],
        compiler_params=pltpu.CompilerParams(vmem_limit_bytes=61 * 1024 * 1024),
    )(*results)


def solution(mesh):
    return jax.shard_map(
        shards,
        mesh=mesh,
        in_specs=(
            P(("shot", "slab"), "side", None),
            P(("shot", "slab"), "side", None),
            P(("shot", "slab"), "side", None),
            P("shot"),
            P("shot"),
            P("shot", None),
            P("shot"),
            P("shot"),
        ),
        out_specs=(
            P(("shot", "slab"), "side", None),
            P(("shot", "slab"), "side", None),
            P(("shot", "slab"), None, "side", None),
        ),
        check_vma=False,
    )
```
